1024 devices in a mesh: rep: 8 (over x, y_lo), exp: 32 (over z, core), node: 4 (over y_hi).
Axes of the slice: x: 4, y: 8 (y_hi: 4, y_lo: 2; y = y_hi * 2 + y_lo), z: 16, core: 2. Of those that a mesh axis runs over, the one named last changes fastest.
Arguments:
- grad_out: bfloat16 [16384, 1664], P(('exp', 'node')), may hold values from -4 to 4
- gates: float32 [16384, 2], P(('exp', 'node')), may hold values from 0.2 to 1
- expert_ids: int32 [16384, 2], P(('exp', 'node')), may hold values from 0 to 31, all different within a row
- saved_inputs: bfloat16 [32, 4, 320, 1664], P('exp', 'node'), may hold values from -6 to 6
- w_in: bfloat16 [32, 1664, 4096], P('exp', None, 'rep'), may hold values from -0.15625 to 0.15625
- w_out: bfloat16 [32, 1664, 4096], P('exp', None, 'rep'), may hold values from -0.09375 to 0.09375
Outputs:
- grad_inputs: bfloat16 [16384, 1664], P(('exp', 'node'), 'rep')
- grad_w_in: bfloat16 [32, 1664, 4096], P('exp', 'node', 'rep')
- grad_w_out: bfloat16 [32, 1664, 4096], P('exp', 'node', 'rep')
The draws below stay inside these ranges and needn't reach their ends.
Inputs may be any that keep to these rules, and one draw needn't show every extreme that they name: `expert_ids`: each patch names 2 different experts, and every expert is named by some patch.
All inputs are finite; a program needn't handle non-finite values.
Results may differ from the reference program's by a relative error of at most 0.013.
Values may be sent and summed in bfloat16 or wider, within the bound.
No kernel may reach another device: no remote copies, remote signals or barrier semaphores. Data moves between devices by JAX's collectives and lax.ppermute only.
A program may use at most 64 MiB of HBM per device.

```python
import jax
import jax.numpy as jnp
from jax import lax

D = 1664
TOP = 2
FF = 4096
TOK_DEV = 128
EXPERTS = 32
TOKENS = 16384
CAP = 10
N_REP = 8
N_EXP = 32
N_NODE = 4


def level_of(rng, extent, split, low, top_value):
    factor_of = 1.0
    for position, shards_of in split:
        heights = jax.random.uniform(jax.random.fold_in(jax.random.fold_in(rng, 6), position), (shards_of,), jnp.float32, low / len(split), top_value / len(split))
        factor_of = factor_of * jnp.repeat(jnp.exp(heights), extent[position] // shards_of).reshape((-1,) + (1,) * (len(extent) - 1 - position))
    return factor_of


def choose_distinct(key, rows, number_of, top, lift):
    sequence = jax.random.permutation(jax.random.fold_in(key, 1), number_of)
    boost = sequence
    for power in range(3):
        boost = boost * boost // number_of
    boost = boost * lift // number_of
    lots = jax.random.randint(jax.random.fold_in(key, 2), (rows, number_of), 0, 4096) + boost
    sure = jax.random.permutation(jax.random.fold_in(key, 3), rows)[jnp.arange(number_of) % rows]
    lots = jnp.where(jnp.arange(rows)[:, None] == sure[None, :], 1 << 14, lots)
    priority = lots * number_of + jnp.arange(number_of)
    return lax.top_k(priority.astype(jnp.int32), top)[1].astype(jnp.int32)


def normal_values(rng, dims, width, bound, cuts=(), held_as=jnp.bfloat16):
    drawn = width * jax.random.normal(rng, dims, jnp.float32)
    if cuts:
        drawn = drawn * level_of(rng, dims, cuts, -0.22, 0.18)
    return jnp.clip(drawn, -bound, bound).astype(held_as)


def setup_inputs(seed: int = 0) -> dict:
    key_list = jax.random.split(jax.random.key(seed), 7)
    return {
        "grad_out": normal_values(key_list[0], (TOKENS, D), 0.5, 4.0, ((0, 128),)),
        "gates": jnp.clip(0.2 + 0.8 * jax.random.uniform(key_list[1], (TOKENS, TOP), jnp.float32) ** level_of(key_list[1], (TOKENS, TOP), ((0, 128),), -0.2, 0.2), 0.2, 1.0),
        "expert_ids": choose_distinct(key_list[2], TOKENS, EXPERTS, TOP, 1024),
        "saved_inputs": normal_values(key_list[3], (EXPERTS, N_NODE, N_EXP * CAP, D), 1.0, 6.0, ((0, 32), (1, 4))),
        "w_in": normal_values(key_list[4], (EXPERTS, D, FF), D ** -0.5, 0.15625, ((0, 32), (2, 8))),
        "w_out": normal_values(key_list[5], (EXPERTS, D, FF), FF ** -0.5, 0.09375, ((0, 32), (2, 8))),
    }


SQRT_HALF = 0.7071067811865476
INV_ROOT_TAU = 0.3989422804014327


def gelu_pair(hidden):
    cdf = 0.5 * (1.0 + lax.erf(hidden * SQRT_HALF))
    return hidden * cdf, cdf + hidden * INV_ROOT_TAU * jnp.exp(-0.5 * hidden * hidden)


def slot_table(ids_group):
    flat = ids_group.T.reshape(-1).astype(jnp.int32)
    onehot = (flat[:, None] == jnp.arange(EXPERTS, dtype=jnp.int32)[None, :]).astype(jnp.int32)
    ranks = jnp.cumsum(onehot, axis=0).astype(jnp.int32) - onehot
    slot = jnp.sum(ranks * onehot, axis=1).astype(jnp.int32)
    return flat, slot, slot < CAP


def dispatch_group(dy_group, gate_group, ids_group):
    flat, slot, kept = slot_table(ids_group)
    target = jnp.where(kept, flat * CAP + slot, -1).astype(jnp.int32)
    places = jnp.arange(EXPERTS * CAP, dtype=jnp.int32)
    match = target[None, :] == places[:, None]
    filled = jnp.any(match, axis=1)
    positions = jnp.arange(TOP * TOK_DEV, dtype=jnp.int32)
    owner = jnp.sum(jnp.where(match, positions[None, :], 0), axis=1).astype(jnp.int32)
    token = owner % TOK_DEV
    column = owner // TOK_DEV
    scale = gate_group[token, column]
    rows = scale[:, None] * dy_group[token].astype(jnp.float32)
    rows = jnp.where(filled[:, None], rows, 0.0).astype(jnp.bfloat16)
    return rows.reshape(EXPERTS, CAP, D)


def expert_grads(operands):
    inputs, upstream, w_in_e, w_out_e = operands
    rows = N_EXP * CAP
    flat_in = inputs.reshape(N_NODE * rows, D)
    flat_up = upstream.reshape(N_NODE * rows, D)
    hidden = jnp.dot(flat_in, w_in_e, preferred_element_type=jnp.float32)
    act, slope = gelu_pair(hidden)
    act = act.astype(jnp.bfloat16)
    dact = jnp.dot(flat_up, w_out_e, preferred_element_type=jnp.float32)
    dhid = (dact * slope).astype(jnp.bfloat16)
    block = FF // N_REP
    partial_value = jnp.zeros((N_NODE * rows, D), jnp.float32)
    for index in range(N_REP):
        piece = jnp.dot(dhid[:, index * block:(index + 1) * block], w_in_e[:, index * block:(index + 1) * block].T, preferred_element_type=jnp.float32).astype(jnp.bfloat16)
        partial_value = partial_value + lax.optimization_barrier(piece).astype(jnp.float32)
    grad_a = jnp.zeros((D, FF), jnp.float32)
    grad_b = jnp.zeros((D, FF), jnp.float32)
    for index in range(N_NODE):
        lower = index * rows
        term_a = jnp.dot(flat_in[lower:lower + rows].T, dhid[lower:lower + rows], preferred_element_type=jnp.float32).astype(jnp.bfloat16)
        term_b = jnp.dot(flat_up[lower:lower + rows].T, act[lower:lower + rows], preferred_element_type=jnp.float32).astype(jnp.bfloat16)
        term_a, term_b = lax.optimization_barrier((term_a, term_b))
        grad_a = grad_a + term_a.astype(jnp.float32)
        grad_b = grad_b + term_b.astype(jnp.float32)
    return partial_value, grad_a.astype(jnp.bfloat16), grad_b.astype(jnp.bfloat16)


def combine_group(back, ids_group):
    flat, slot, kept = slot_table(ids_group)
    index = jnp.where(kept, flat * CAP + slot, 0).astype(jnp.int32)
    values = jnp.where(kept[:, None], back[index], 0.0)
    return jnp.sum(values.reshape(TOP, TOK_DEV, D), axis=0)


def reference(grad_out, gates, expert_ids, saved_inputs, w_in, w_out):
    groups = N_EXP * N_NODE
    rows = N_EXP * CAP
    sent = jax.vmap(dispatch_group)(grad_out.reshape(groups, TOK_DEV, D), gates.reshape(groups, TOK_DEV, TOP), expert_ids.reshape(groups, TOK_DEV, TOP))
    upstream = sent.reshape(N_EXP, N_NODE, EXPERTS, CAP, D).transpose(2, 1, 0, 3, 4).reshape(EXPERTS, N_NODE, rows, D)
    partial_value, grad_w_in, grad_w_out = lax.map(expert_grads, (saved_inputs, upstream, w_in, w_out))
    back = partial_value.reshape(EXPERTS, N_NODE, N_EXP, CAP, D).transpose(2, 1, 0, 3, 4).reshape(groups, EXPERTS * CAP, D)
    merged = jax.vmap(combine_group)(back, expert_ids.reshape(groups, TOK_DEV, TOP))
    return merged.reshape(TOKENS, D).astype(jnp.bfloat16), grad_w_in, grad_w_out
```

```python
import jax
import jax.numpy as jnp
from jax import lax
from jax.experimental import pallas as pl
from jax.experimental.pallas import tpu as pltpu
from jax.sharding import PartitionSpec as P

SQRT_HALF = 0.7071067811865476
INV_ROOT_TAU = 0.3989422804014327

REP, EXP, NODE = 8, 32, 4
TOK, WIDTH, CAP = 128, 1664, 10
SLOTS = EXP * CAP
HID = 512
LANES = 128
TILES = WIDTH // LANES
COLS = WIDTH // REP
ROWS = WIDTH // NODE
SENDS = EXP // REP
PACKED = 136
BACK = 24
SHARE = SENDS * CAP

VMEM = pl.BlockSpec(memory_space=pltpu.VMEM)
SMEM = pl.BlockSpec(memory_space=pltpu.SMEM)
PARAMS = pltpu.CompilerParams(vmem_limit_bytes=48 * 1024 * 1024)


def iota(shape, dim):
    return lax.broadcasted_iota(jnp.int32, shape, dim)


def hot(mask):
    return jnp.where(mask, 1.0, 0.0).astype(jnp.bfloat16)


def dot(a, b, dims=((1,), (0,))):
    return lax.dot_general(a, b, (dims, ((), ())), preferred_element_type=jnp.float32)


def dispatch_kernel(pos_ref, ids_ref, gates_ref, grad_ref, o0, o1, o2, o3, code_ref):
    rep, src = pos_ref[0], pos_ref[1]
    lane = iota((TOK, LANES), 1)
    before = hot(iota((TOK, TOK), 0) > iota((TOK, TOK), 1))
    first = ids_ref[:, 0:1]
    second = ids_ref[:, 1:2]
    hot0 = hot(first == lane)
    hot1 = hot(second == lane)
    count0 = jnp.sum(hot0.astype(jnp.float32), axis=0, keepdims=True)
    rank0 = dot(before, hot0)
    rank1 = dot(before, hot1) + count0
    slot0 = jnp.sum(rank0 * hot0.astype(jnp.float32), axis=1, keepdims=True).astype(jnp.int32)
    slot1 = jnp.sum(rank1 * hot1.astype(jnp.float32), axis=1, keepdims=True).astype(jnp.int32)
    kept0 = slot0 < CAP
    kept1 = slot1 < CAP
    code_ref[:, 0:1] = jnp.where(kept0, first * BACK + slot0, -100)
    code_ref[:, 1:2] = jnp.where(kept1, second * BACK + slot1, -100)
    target0 = jnp.where(kept0, first * 16 + slot0, -1)
    target1 = jnp.where(kept1, second * 16 + slot1, -1)
    col = iota((1, LANES), 1)
    k = col >> 4
    c = col & 15
    expert = ((rep - src) & 7) + 8 * (((src >> 3) + k) & 3)
    wanted = jnp.where((c < CAP) & (k < SENDS), expert * 16 + c, -2)
    grad = grad_ref[...].astype(jnp.float32)
    scaled0 = (gates_ref[:, 0:1] * grad).astype(jnp.bfloat16)
    scaled1 = (gates_ref[:, 1:2] * grad).astype(jnp.bfloat16)
    rows = dot(hot(target0 == wanted), scaled0, ((0,), (0,))) + dot(
        hot(target1 == wanted), scaled1, ((0,), (0,))
    )
    rows = rows.astype(jnp.bfloat16)
    stacked = jnp.concatenate(
        [
            jnp.concatenate(
                [rows[16 * q : 16 * q + 16, LANES * t : LANES * (t + 1)] for q in range(SENDS)],
                axis=1,
            )
            for t in range(TILES)
        ],
        axis=0,
    )
    i = iota((PACKED, 16 * TILES), 1)
    squeeze = hot((iota((PACKED, 16 * TILES), 0) == (i >> 4) * CAP + (i & 15)) & ((i & 15) < CAP))
    packed = dot(squeeze, stacked).astype(jnp.bfloat16)
    for q, out in enumerate((o0, o1, o2, o3)):
        out[...] = packed[:, LANES * q : LANES * (q + 1)]


def unpack_kernel(i0, i1, i2, i3, out_ref):
    packed = jnp.concatenate([ref[...] for ref in (i0, i1, i2, i3)], axis=1)
    i = iota((16 * TILES, PACKED), 0)
    spread = hot((iota((16 * TILES, PACKED), 1) == (i >> 4) * CAP + (i & 15)) & ((i & 15) < CAP))
    stacked = dot(spread, packed).astype(jnp.bfloat16)
    rows = jnp.concatenate(
        [
            jnp.concatenate(
                [stacked[16 * t : 16 * t + 16, LANES * q : LANES * (q + 1)] for t in range(TILES)],
                axis=1,
            )
            for q in range(SENDS)
        ],
        axis=0,
    )
    j = iota((SHARE, 16 * SENDS), 0)
    k = lax.div(j, CAP)
    dense = hot(iota((SHARE, 16 * SENDS), 1) == k * 16 + (j - k * CAP))
    share = dot(dense, rows).astype(jnp.bfloat16)
    for q in range(REP):
        out_ref[q] = share


def middle_kernel(pos_ref, got_ref, w_in_ref, w_out_ref, slope_ref, up_ref, dhid_ref, part_ref):
    exp = pos_ref[1]
    j = iota((1, SLOTS), 1)
    block = lax.div(j, SHARE)
    rest = j - block * SHARE
    k = lax.div(rest, CAP)
    source = ((block - exp) & 7) + 8 * (((exp >> 3) - k) & 3)
    place = source * CAP + (rest - k * CAP)
    up = dot(hot(iota((SLOTS, SLOTS), 0) == place), got_ref[...]).astype(jnp.bfloat16)
    up_ref[...] = up
    dhid = (dot(up, w_out_ref[...]) * slope_ref[...]).astype(jnp.bfloat16)
    for q in range(NODE):
        dhid_ref[q] = dhid
    for q in range(REP):
        part_ref[q] = dot(dhid, w_in_ref[COLS * q : COLS * (q + 1), :], ((1,), (1,))).astype(
            jnp.bfloat16
        )


def back_kernel(part_ref, out_ref):
    total = part_ref[0].astype(jnp.float32)
    for q in range(1, REP):
        total = total + part_ref[q].astype(jnp.float32)
    total = total.astype(jnp.bfloat16)
    tail = dot(total, hot(iota((COLS, LANES), 0) == iota((COLS, LANES), 1) + LANES))
    m = iota((EXP * BACK, SLOTS), 0)
    s = lax.div(m, BACK)
    q = m - s * BACK
    j = iota((EXP * BACK, SLOTS), 1)
    one = hot((j == s * CAP + q) & (q < CAP))
    two = hot((j == s * CAP + q - CAP) & (q >= CAP) & (q < 2 * CAP))
    out = dot(one, total[:, :LANES]) + dot(two, tail.astype(jnp.bfloat16))
    out_ref[...] = out.astype(jnp.bfloat16)


def combine_kernel(code_ref, back_ref, out_ref):
    lane = iota((TOK, EXP * BACK), 1)
    code0 = code_ref[:, 0:1]
    code1 = code_ref[:, 1:2]
    back = back_ref[...]
    head = dot(hot((lane == code0) | (lane == code1)), back)
    tail = dot(hot((lane == code0 + CAP) | (lane == code1 + CAP)), back)
    out_ref[:, :LANES] = head.astype(jnp.bfloat16)
    out_ref[:, LANES:] = tail[:, : COLS - LANES].astype(jnp.bfloat16)


def call(kernel, out, in_specs, *args):
    return pl.pallas_call(
        kernel,
        out_shape=out,
        in_specs=in_specs,
        out_specs=jax.tree.map(lambda _: VMEM, out),
        compiler_params=PARAMS,
    )(*args)


def shape(*dims, dtype=jnp.bfloat16):
    return jax.ShapeDtypeStruct(dims, dtype)


def send_pairs(k):
    pairs = []
    for rep in range(REP):
        for src in range(EXP):
            dst = (rep - src) % 8 + 8 * ((src // 8 + k) % SENDS)
            pairs.append((rep * EXP + src, rep * EXP + dst))
    return pairs


def local(grad_out, gates, expert_ids, saved_inputs, w_in, w_out):
    pos = jnp.stack([lax.axis_index("rep"), lax.axis_index("exp")]).astype(jnp.int32)
    inputs = saved_inputs[0, 0]
    proj_in = w_in[0]
    proj_out = w_out[0]

    *packed, code = call(
        dispatch_kernel,
        [shape(PACKED, LANES)] * SENDS + [shape(TOK, 2, dtype=jnp.int32)],
        [SMEM] + [VMEM] * 3,
        pos,
        expert_ids,
        gates,
        grad_out,
    )
    landed = [lax.ppermute(p, ("rep", "exp"), send_pairs(k)) for k, p in enumerate(packed)]

    hidden = dot(inputs, proj_in)
    cdf = 0.5 * (1.0 + lax.erf(hidden * SQRT_HALF))
    act = (hidden * cdf).astype(jnp.bfloat16)
    slope = cdf + hidden * INV_ROOT_TAU * jnp.exp(-0.5 * hidden * hidden)
    input_cols = lax.all_to_all(
        inputs.reshape(SLOTS, NODE, ROWS).transpose(1, 0, 2), "node", 0, 0, tiled=True
    )

    shares = call(unpack_kernel, shape(REP, SHARE, WIDTH), [VMEM] * SENDS, *landed)
    got = lax.all_to_all(shares, "rep", 0, 0, tiled=True).reshape(SLOTS, WIDTH)
    up, dhid, part = call(
        middle_kernel,
        [shape(SLOTS, WIDTH), shape(NODE, SLOTS, HID), shape(REP, SLOTS, COLS)],
        [SMEM] + [VMEM] * 4,
        pos,
        got,
        proj_in,
        proj_out,
        slope,
    )
    part = lax.all_to_all(part, "rep", 0, 0, tiled=True)
    dhid_all = lax.all_to_all(dhid, "node", 0, 0, tiled=True)
    grad_b = dot(up, act, ((0,), (0,))).astype(jnp.bfloat16)
    grad_w_out = lax.psum_scatter(grad_b, "node", scatter_dimension=0, tiled=True)

    back = call(back_kernel, shape(EXP * BACK, LANES), [VMEM], part)
    back = lax.all_to_all(back.reshape(EXP, BACK, LANES), "exp", 0, 0, tiled=True)
    grad_inputs = call(
        combine_kernel, shape(TOK, COLS), [VMEM] * 2, code, back.reshape(EXP * BACK, LANES)
    )
    grad_w_in = dot(
        input_cols.reshape(NODE * SLOTS, ROWS), dhid_all.reshape(NODE * SLOTS, HID), ((0,), (0,))
    ).astype(jnp.bfloat16)
    return grad_inputs, grad_w_in[None], grad_w_out[None]


def solution(mesh):
    return jax.shard_map(
        local,
        mesh=mesh,
        in_specs=(
            P(("exp", "node"), None),
            P(("exp", "node"), None),
            P(("exp", "node"), None),
            P("exp", "node", None, None),
            P("exp", None, "rep"),
            P("exp", None, "rep"),
        ),
        out_specs=(P(("exp", "node"), "rep"), P("exp", "node", "rep"), P("exp", "node", "rep")),
        check_vma=False,
    )
```

```python
import jax
import jax.numpy as jnp
from jax import lax
from jax.experimental import pallas as pl
from jax.experimental.pallas import tpu as pltpu
from jax.sharding import PartitionSpec as P

SQRT_HALF = 0.7071067811865476
INV_ROOT_TAU = 0.3989422804014327

REP, EXP, NODE = 8, 32, 4
TOK, WIDTH, CAP = 128, 1664, 10
SLOTS = EXP * CAP
HID = 512
LANES = 128
TILES = WIDTH // LANES
COLS = WIDTH // REP
ROWS = WIDTH // NODE
SENDS = EXP // REP
PACKED = 136
BACK = 24
HALF = LANES // 2
PART = 528
SHARE = SENDS * CAP
ORDER = (2, 1, 3, 0)

VMEM = pl.BlockSpec(memory_space=pltpu.VMEM)
SMEM = pl.BlockSpec(memory_space=pltpu.SMEM)
HBM = pl.BlockSpec(memory_space=pltpu.HBM)
PARAMS = pltpu.CompilerParams(vmem_limit_bytes=48 * 1024 * 1024)


def iota(shape, dim):
    return lax.broadcasted_iota(jnp.int32, shape, dim)


def hot(mask):
    return jnp.where(mask, 1.0, 0.0).astype(jnp.bfloat16)


def dot(a, b, dims=((1,), (0,))):
    return lax.dot_general(a, b, (dims, ((), ())), preferred_element_type=jnp.float32)


def in_order(k):
    step = jnp.full_like(k, ORDER[0])
    for q in range(1, SENDS):
        step = jnp.where(k == q, ORDER[q], step)
    return step


def dispatch_kernel(pos_ref, ids_ref, gates_ref, grad_ref, o0, o1, o2, o3, code_ref):
    rep, src = pos_ref[0], pos_ref[1]
    lane = iota((TOK, LANES), 1)
    before = hot(iota((TOK, TOK), 0) > iota((TOK, TOK), 1))
    ids = jnp.concatenate([ids_ref[...], jnp.zeros((6, TOK), jnp.int32)], axis=0).T
    gates = jnp.concatenate([gates_ref[...], jnp.zeros((6, TOK), jnp.float32)], axis=0).T
    first = ids[:, 0:1]
    second = ids[:, 1:2]
    hot0 = hot(first == lane)
    hot1 = hot(second == lane)
    count0 = jnp.sum(hot0.astype(jnp.float32), axis=0, keepdims=True)
    rank0 = dot(before, hot0)
    rank1 = dot(before, hot1) + count0
    slot0 = jnp.sum(rank0 * hot0.astype(jnp.float32), axis=1, keepdims=True).astype(jnp.int32)
    slot1 = jnp.sum(rank1 * hot1.astype(jnp.float32), axis=1, keepdims=True).astype(jnp.int32)
    kept0 = slot0 < CAP
    kept1 = slot1 < CAP
    code_ref[:, 0:1] = jnp.where(kept0, first * BACK + slot0, -100)
    code_ref[:, 1:2] = jnp.where(kept1, second * BACK + slot1, -100)
    target0 = jnp.where(kept0, first * 16 + slot0, -1)
    target1 = jnp.where(kept1, second * 16 + slot1, -1)
    col = iota((1, LANES), 1)
    k = col >> 4
    c = col & 15
    expert = ((rep - src) & 7) + 8 * (((src >> 3) + in_order(k)) & 3)
    wanted = jnp.where((c < CAP) & (k < SENDS), expert * 16 + c, -2)
    grad = grad_ref[...].astype(jnp.float32)
    scaled0 = (gates[:, 0:1] * grad).astype(jnp.bfloat16)
    scaled1 = (gates[:, 1:2] * grad).astype(jnp.bfloat16)
    rows = dot(hot(target0 == wanted), scaled0, ((0,), (0,))) + dot(
        hot(target1 == wanted), scaled1, ((0,), (0,))
    )
    rows = rows.astype(jnp.bfloat16)
    stacked = jnp.concatenate(
        [
            jnp.concatenate(
                [rows[16 * q : 16 * q + 16, LANES * t : LANES * (t + 1)] for q in range(SENDS)],
                axis=1,
            )
            for t in range(TILES)
        ],
        axis=0,
    )
    i = iota((PACKED, 16 * TILES), 1)
    squeeze = hot((iota((PACKED, 16 * TILES), 0) == (i >> 4) * CAP + (i & 15)) & ((i & 15) < CAP))
    packed = dot(squeeze, stacked).astype(jnp.bfloat16)
    for q, out in enumerate((o0, o1, o2, o3)):
        out[...] = packed[:, LANES * q : LANES * (q + 1)]


def unpack_kernel(i0, i1, i2, i3, out_ref):
    packed = jnp.concatenate([ref[...] for ref in (i0, i1, i2, i3)], axis=1)
    i = iota((16 * TILES, PACKED), 0)
    spread = hot((iota((16 * TILES, PACKED), 1) == (i >> 4) * CAP + (i & 15)) & ((i & 15) < CAP))
    stacked = dot(spread, packed).astype(jnp.bfloat16)
    rows = jnp.concatenate(
        [
            jnp.concatenate(
                [stacked[16 * t : 16 * t + 16, LANES * q : LANES * (q + 1)] for t in range(TILES)],
                axis=1,
            )
            for q in range(SENDS)
        ],
        axis=0,
    )
    j = iota((SHARE, 16 * SENDS), 0)
    k = lax.div(j, CAP)
    dense = hot(iota((SHARE, 16 * SENDS), 1) == k * 16 + (j - k * CAP))
    share = dot(dense, rows).astype(jnp.bfloat16)
    for q in range(REP):
        out_ref[q] = share


def fold(rows):
    half = rows.shape[0] // 2
    return jnp.concatenate([rows[:half], rows[half:]], axis=1)


def unfold(rows):
    return jnp.concatenate([rows[:, :HALF], rows[:, HALF:]], axis=0)


def landing(exp):
    j = iota((1, SLOTS), 1)
    block = lax.div(j, SHARE)
    rest = j - block * SHARE
    k = lax.div(rest, CAP)
    source = ((block - exp) & 7) + 8 * (((exp >> 3) - in_order(k)) & 3)
    return hot(iota((SLOTS, SLOTS), 0) == source * CAP + (rest - k * CAP))


def hidden_kernel(inputs_ref, w_in_ref, act_ref, slope_ref, wide_ref):
    inputs = inputs_ref[...]
    hidden = dot(inputs, w_in_ref[...])
    cdf = 0.5 * (1.0 + lax.erf(hidden * SQRT_HALF))
    act_ref[...] = (hidden * cdf).astype(jnp.bfloat16)
    slope_ref[...] = cdf + hidden * INV_ROOT_TAU * jnp.exp(-0.5 * hidden * hidden)
    wide_ref[...] = inputs.T


def middle_kernel(
    pos_ref, got_ref, wide_ref, act_ref, w_out_ref, w_in_ref, slope_ref,
    part_ref, terms_hbm, terms_ref, sems,
):
    up = dot(landing(pos_ref[1]), got_ref[...]).astype(jnp.bfloat16)
    dhid = (dot(up, w_out_ref[...]) * slope_ref[...]).astype(jnp.bfloat16)
    copies = []
    for q in range(NODE):
        rows = slice(ROWS * q, ROWS * (q + 1))
        terms_ref[q, :ROWS] = dot(wide_ref[rows, :], dhid).astype(jnp.bfloat16)
    term = dot(up, act_ref[...], ((0,), (0,)))
    for q in range(NODE):
        terms_ref[q, ROWS:] = term[ROWS * q : ROWS * (q + 1)].astype(jnp.bfloat16)
        copies.append(pltpu.make_async_copy(terms_ref.at[q], terms_hbm.at[q], sems.at[q]))
        copies[-1].start()
    for q in range(REP):
        block = dot(w_in_ref[COLS * q : COLS * (q + 1), :], dhid, ((1,), (1,)))
        part_ref[q, 0:COLS] = block[:, :LANES].astype(jnp.bfloat16)
        part_ref[q, COLS : 2 * COLS] = block[:, LANES : 2 * LANES].astype(jnp.bfloat16)
        last = fold(block[:, 2 * LANES :])
        last = jnp.concatenate([last, jnp.zeros((8, LANES), jnp.float32)], axis=0)
        part_ref[q, 2 * COLS :] = last.astype(jnp.bfloat16)
    for copy in copies:
        copy.wait()


def back_kernel(part_ref, out_ref):
    total = part_ref[0].astype(jnp.float32)
    for q in range(1, REP):
        total = total + part_ref[q].astype(jnp.float32)
    last = unfold(total[2 * COLS : 2 * COLS + COLS // 2])
    total = jnp.concatenate([total[:COLS], total[COLS : 2 * COLS]], axis=1)
    total = jnp.concatenate([total, last], axis=1)
    total = jnp.concatenate([total, jnp.zeros((2 * LANES - COLS, SLOTS), jnp.float32)], axis=0)
    total = total.astype(jnp.bfloat16)
    m = iota((EXP * BACK, SLOTS), 0)
    s = lax.div(m, BACK)
    q = m - s * BACK
    j = iota((EXP * BACK, SLOTS), 1)
    one = hot((j == s * CAP + q) & (q < CAP))
    two = hot((j == s * CAP + q - CAP) & (q >= CAP) & (q < 2 * CAP))
    out = dot(one, total[:LANES], ((1,), (1,))) + dot(two, total[LANES:], ((1,), (1,)))
    out_ref[...] = out.astype(jnp.bfloat16)


def combine_kernel(code_ref, back_ref, out_ref):
    lane = iota((TOK, EXP * BACK), 1)
    code0 = code_ref[:, 0:1]
    code1 = code_ref[:, 1:2]
    back = back_ref[...]
    head = dot(back, hot((lane == code0) | (lane == code1)), ((0,), (1,)))
    tail = dot(back, hot((lane == code0 + CAP) | (lane == code1 + CAP)), ((0,), (1,)))
    out_ref[:LANES] = head.astype(jnp.bfloat16)
    out_ref[LANES:] = tail[: COLS - LANES].astype(jnp.bfloat16)


def call(kernel, out, in_specs, *args, scratch=(), out_specs=None):
    return pl.pallas_call(
        kernel,
        out_shape=out,
        in_specs=in_specs,
        out_specs=out_specs or jax.tree.map(lambda _: VMEM, out),
        scratch_shapes=list(scratch),
        compiler_params=PARAMS,
    )(*args)


def shape(*dims, dtype=jnp.bfloat16):
    return jax.ShapeDtypeStruct(dims, dtype)


def send_pairs(k):
    pairs = []
    for rep in range(REP):
        for src in range(EXP):
            dst = (rep - src) % 8 + 8 * ((src // 8 + k) % SENDS)
            pairs.append((rep * EXP + src, rep * EXP + dst))
    return pairs


def local(grad_out, gates, expert_ids, saved_inputs, w_in, w_out):
    pos = jnp.stack([lax.axis_index("rep"), lax.axis_index("exp"), lax.axis_index("node")])
    pos = pos.astype(jnp.int32)
    inputs = saved_inputs[0, 0]
    proj_in = w_in[0]
    proj_out = w_out[0]

    *packed, code = call(
        dispatch_kernel,
        [shape(PACKED, LANES)] * SENDS + [shape(TOK, 2, dtype=jnp.int32)],
        [SMEM] + [VMEM] * 3,
        pos,
        expert_ids.T,
        gates.T,
        grad_out,
    )
    landed = [lax.ppermute(p, ("rep", "exp"), send_pairs(k)) for k, p in zip(ORDER, packed)]

    act, slope, wide = call(
        hidden_kernel,
        [shape(SLOTS, HID), shape(SLOTS, HID, dtype=jnp.float32), shape(WIDTH, SLOTS)],
        [VMEM] * 2,
        inputs,
        proj_in,
    )

    *landed, slope, wide, act = lax.optimization_barrier((*landed, slope, wide, act))
    shares = call(unpack_kernel, shape(REP, SHARE, WIDTH), [VMEM] * SENDS, *landed)
    got = lax.all_to_all(shares, "rep", 0, 0, tiled=True).reshape(SLOTS, WIDTH)
    part, terms = call(
        middle_kernel,
        [shape(REP, PART, LANES), shape(NODE, 2 * ROWS, HID)],
        [SMEM] + [VMEM] * 6,
        pos,
        got,
        wide,
        act,
        proj_out,
        proj_in,
        slope,
        scratch=[
            pltpu.VMEM((NODE, 2 * ROWS, HID), jnp.bfloat16),
            pltpu.SemaphoreType.DMA((NODE,)),
        ],
        out_specs=[VMEM, HBM],
    )
    summed = lax.psum_scatter(
        terms.reshape(NODE * 2 * ROWS, HID), "node", scatter_dimension=0, tiled=True
    )
    part = lax.all_to_all(part, "rep", 0, 0, tiled=True)

    back = call(back_kernel, shape(EXP * BACK, LANES), [VMEM], part)
    back = lax.all_to_all(back.reshape(EXP, BACK, LANES), "exp", 0, 0, tiled=True)
    grad_inputs = call(
        combine_kernel, shape(COLS, TOK), [VMEM] * 2, code, back.reshape(EXP * BACK, LANES)
    )
    return grad_inputs.T, summed[None, :ROWS], summed[None, ROWS:]


def solution(mesh):
    return jax.shard_map(
        local,
        mesh=mesh,
        in_specs=(
            P(("exp", "node"), None),
            P(("exp", "node"), None),
            P(("exp", "node"), None),
            P("exp", "node", None, None),
            P("exp", None, "rep"),
            P("exp", None, "rep"),
        ),
        out_specs=(P(("exp", "node"), "rep"), P("exp", "node", "rep"), P("exp", "node", "rep")),
        check_vma=False,
    )
```

```python
import jax
import jax.numpy as jnp
from jax import lax
from jax.experimental import pallas as pl
from jax.experimental.pallas import tpu as pltpu
from jax.sharding import PartitionSpec as P

SQRT_HALF = 0.7071067811865476
INV_ROOT_TAU = 0.3989422804014327

REP, EXP, NODE = 8, 32, 4
X, PAIR = 4, 2
ALONG_X = [[PAIR * x + y for x in range(X)] for y in range(PAIR)]
NEIGHBOUR = [(r, r ^ 1) for r in range(REP)]
TOK, WIDTH, CAP = 128, 1664, 10
SLOTS = EXP * CAP
HID = 512
LANES = 128
TILES = WIDTH // LANES
COLS = WIDTH // REP
ROWS = WIDTH // NODE
SENDS = EXP // REP
PACKED = 136
BACK = 24
HALF = LANES // 2
PART = 528
SHARE = SENDS * CAP
ORDER = (2, 1, 3, 0)

VMEM = pl.BlockSpec(memory_space=pltpu.VMEM)
SMEM = pl.BlockSpec(memory_space=pltpu.SMEM)
HBM = pl.BlockSpec(memory_space=pltpu.HBM)
PARAMS = pltpu.CompilerParams(vmem_limit_bytes=48 * 1024 * 1024)


def iota(shape, dim):
    return lax.broadcasted_iota(jnp.int32, shape, dim)


def hot(mask):
    return jnp.where(mask, 1.0, 0.0).astype(jnp.bfloat16)


def dot(a, b, dims=((1,), (0,))):
    return lax.dot_general(a, b, (dims, ((), ())), preferred_element_type=jnp.float32)


def in_order(k):
    step = jnp.full_like(k, ORDER[0])
    for q in range(1, SENDS):
        step = jnp.where(k == q, ORDER[q], step)
    return step


def dispatch_kernel(pos_ref, ids_ref, gates_ref, grad_ref, o0, o1, o2, o3, code_ref):
    rep, src = pos_ref[0], pos_ref[1]
    lane = iota((TOK, LANES), 1)
    before = hot(iota((TOK, TOK), 0) > iota((TOK, TOK), 1))
    ids = jnp.concatenate([ids_ref[...], jnp.zeros((6, TOK), jnp.int32)], axis=0).T
    gates = jnp.concatenate([gates_ref[...], jnp.zeros((6, TOK), jnp.float32)], axis=0).T
    first = ids[:, 0:1]
    second = ids[:, 1:2]
    hot0 = hot(first == lane)
    hot1 = hot(second == lane)
    count0 = jnp.sum(hot0.astype(jnp.float32), axis=0, keepdims=True)
    rank0 = dot(before, hot0)
    rank1 = dot(before, hot1) + count0
    slot0 = jnp.sum(rank0 * hot0.astype(jnp.float32), axis=1, keepdims=True).astype(jnp.int32)
    slot1 = jnp.sum(rank1 * hot1.astype(jnp.float32), axis=1, keepdims=True).astype(jnp.int32)
    kept0 = slot0 < CAP
    kept1 = slot1 < CAP
    code_ref[:, 0:1] = jnp.where(kept0, first * BACK + slot0, -100)
    code_ref[:, 1:2] = jnp.where(kept1, second * BACK + slot1, -100)
    target0 = jnp.where(kept0, first * 16 + slot0, -1)
    target1 = jnp.where(kept1, second * 16 + slot1, -1)
    col = iota((1, LANES), 1)
    k = col >> 4
    c = col & 15
    expert = ((rep - src) & 7) + 8 * (((src >> 3) + in_order(k)) & 3)
    wanted = jnp.where((c < CAP) & (k < SENDS), expert * 16 + c, -2)
    grad = grad_ref[...].astype(jnp.float32)
    scaled0 = (gates[:, 0:1] * grad).astype(jnp.bfloat16)
    scaled1 = (gates[:, 1:2] * grad).astype(jnp.bfloat16)
    rows = dot(hot(target0 == wanted), scaled0, ((0,), (0,))) + dot(
        hot(target1 == wanted), scaled1, ((0,), (0,))
    )
    rows = rows.astype(jnp.bfloat16)
    stacked = jnp.concatenate(
        [
            jnp.concatenate(
                [rows[16 * q : 16 * q + 16, LANES * t : LANES * (t + 1)] for q in range(SENDS)],
                axis=1,
            )
            for t in range(TILES)
        ],
        axis=0,
    )
    i = iota((PACKED, 16 * TILES), 1)
    squeeze = hot((iota((PACKED, 16 * TILES), 0) == (i >> 4) * CAP + (i & 15)) & ((i & 15) < CAP))
    packed = dot(squeeze, stacked).astype(jnp.bfloat16)
    for q, out in enumerate((o0, o1, o2, o3)):
        out[...] = packed[:, LANES * q : LANES * (q + 1)]


def unpack_kernel(i0, i1, i2, i3, out_ref):
    packed = jnp.concatenate([ref[...] for ref in (i0, i1, i2, i3)], axis=1)
    i = iota((16 * TILES, PACKED), 0)
    spread = hot((iota((16 * TILES, PACKED), 1) == (i >> 4) * CAP + (i & 15)) & ((i & 15) < CAP))
    stacked = dot(spread, packed).astype(jnp.bfloat16)
    rows = jnp.concatenate(
        [
            jnp.concatenate(
                [stacked[16 * t : 16 * t + 16, LANES * q : LANES * (q + 1)] for t in range(TILES)],
                axis=1,
            )
            for q in range(SENDS)
        ],
        axis=0,
    )
    j = iota((SHARE, 16 * SENDS), 0)
    k = lax.div(j, CAP)
    dense = hot(iota((SHARE, 16 * SENDS), 1) == k * 16 + (j - k * CAP))
    share = dot(dense, rows).astype(jnp.bfloat16)
    for q in range(REP):
        out_ref[q] = share


def fold(rows):
    half = rows.shape[0] // 2
    return jnp.concatenate([rows[:half], rows[half:]], axis=1)


def unfold(rows):
    return jnp.concatenate([rows[:, :HALF], rows[:, HALF:]], axis=0)


def places(exp):
    j = iota((1, SLOTS), 1)
    block = lax.div(j, SHARE)
    rest = j - block * SHARE
    k = lax.div(rest, CAP)
    source = ((block - exp) & 7) + 8 * (((exp >> 3) - in_order(k)) & 3)
    return source * CAP + (rest - k * CAP)


def hidden_kernel(pos_ref, inputs_ref, w_in_ref, act_ref, slope_ref, wide_ref):
    order = hot(iota((SLOTS, SLOTS), 0) == places(pos_ref[1]))
    inputs = dot(order, inputs_ref[...], ((0,), (0,))).astype(jnp.bfloat16)
    hidden = dot(inputs, w_in_ref[...])
    cdf = 0.5 * (1.0 + lax.erf(hidden * SQRT_HALF))
    act_ref[...] = (hidden * cdf).astype(jnp.bfloat16)
    slope_ref[...] = cdf + hidden * INV_ROOT_TAU * jnp.exp(-0.5 * hidden * hidden)
    wide_ref[...] = inputs.T


def middle_kernel(
    got_ref, wide_ref, act_ref, w_out_ref, slope_ref, dhid_ref, terms_hbm, terms_ref, sems
):
    up = got_ref[...]
    dhid = (dot(up, w_out_ref[...]) * slope_ref[...]).astype(jnp.bfloat16)
    dhid_ref[...] = dhid
    term = dot(up, act_ref[...], ((0,), (0,)))
    copies = []
    for q in range(NODE):
        rows = slice(ROWS * q, ROWS * (q + 1))
        terms_ref[q, ROWS:] = term[rows].astype(jnp.bfloat16)
        terms_ref[q, :ROWS] = dot(wide_ref[rows, :], dhid).astype(jnp.bfloat16)
        copies.append(pltpu.make_async_copy(terms_ref.at[q], terms_hbm.at[q], sems.at[q]))
        copies[-1].start()
    for copy in copies:
        copy.wait()


def split_kernel(summed_hbm, in_hbm, out_hbm, sems):
    copies = [
        pltpu.make_async_copy(summed_hbm.at[:ROWS], in_hbm, sems.at[0]),
        pltpu.make_async_copy(summed_hbm.at[ROWS:], out_hbm, sems.at[1]),
    ]
    for copy in copies:
        copy.start()
    for copy in copies:
        copy.wait()


def part_kernel(dhid_ref, w_in_ref, part_ref):
    dhid = dhid_ref[...]
    for q in range(REP):
        block = dot(w_in_ref[COLS * q : COLS * (q + 1), :], dhid, ((1,), (1,)))
        x, y = divmod(q, PAIR)
        part_ref[x, y, 0:COLS] = block[:, :LANES].astype(jnp.bfloat16)
        part_ref[x, y, COLS : 2 * COLS] = block[:, LANES : 2 * LANES].astype(jnp.bfloat16)
        last = fold(block[:, 2 * LANES :])
        last = jnp.concatenate([last, jnp.zeros((8, LANES), jnp.float32)], axis=0)
        part_ref[x, y, 2 * COLS :] = last.astype(jnp.bfloat16)


def sum_kernel(pos_ref, part_ref, keep_ref, send_ref):
    mine = pos_ref[0] & 1
    keep = part_ref[0, mine].astype(jnp.float32)
    send = part_ref[0, 1 - mine].astype(jnp.float32)
    for q in range(1, X):
        keep = keep + part_ref[q, mine].astype(jnp.float32)
        send = send + part_ref[q, 1 - mine].astype(jnp.float32)
    keep_ref[...] = keep
    send_ref[...] = send.astype(jnp.bfloat16)


def back_kernel(pos_ref, keep_ref, other_ref, out_ref):
    total = keep_ref[...] + other_ref[...].astype(jnp.float32)
    last = unfold(total[2 * COLS : 2 * COLS + COLS // 2])
    total = jnp.concatenate([total[:COLS], total[COLS : 2 * COLS]], axis=1)
    total = jnp.concatenate([total, last], axis=1)
    total = jnp.concatenate([total, jnp.zeros((2 * LANES - COLS, SLOTS), jnp.float32)], axis=0)
    total = total.astype(jnp.bfloat16)
    m = iota((EXP * BACK, SLOTS), 0)
    s = lax.div(m, BACK)
    q = m - s * BACK
    place = places(pos_ref[1])
    one = hot((place == s * CAP + q) & (q < CAP))
    two = hot((place == s * CAP + q - CAP) & (q >= CAP) & (q < 2 * CAP))
    out = dot(one, total[:LANES], ((1,), (1,))) + dot(two, total[LANES:], ((1,), (1,)))
    out_ref[...] = out.astype(jnp.bfloat16)


def combine_kernel(code_ref, back_ref, out_ref):
    lane = iota((TOK, EXP * BACK), 1)
    code0 = code_ref[:, 0:1]
    code1 = code_ref[:, 1:2]
    back = back_ref[...]
    head = dot(back, hot((lane == code0) | (lane == code1)), ((0,), (1,)))
    tail = dot(back, hot((lane == code0 + CAP) | (lane == code1 + CAP)), ((0,), (1,)))
    out_ref[:LANES] = head.astype(jnp.bfloat16)
    out_ref[LANES:] = tail[: COLS - LANES].astype(jnp.bfloat16)


def call(kernel, out, in_specs, *args, scratch=(), out_specs=None):
    return pl.pallas_call(
        kernel,
        out_shape=out,
        in_specs=in_specs,
        out_specs=out_specs or jax.tree.map(lambda _: VMEM, out),
        scratch_shapes=list(scratch),
        compiler_params=PARAMS,
    )(*args)


def shape(*dims, dtype=jnp.bfloat16):
    return jax.ShapeDtypeStruct(dims, dtype)


def send_pairs(k):
    pairs = []
    for rep in range(REP):
        for src in range(EXP):
            dst = (rep - src) % 8 + 8 * ((src // 8 + k) % SENDS)
            pairs.append((rep * EXP + src, rep * EXP + dst))
    return pairs


def local(grad_out, gates, expert_ids, saved_inputs, w_in, w_out):
    pos = jnp.stack([lax.axis_index("rep"), lax.axis_index("exp"), lax.axis_index("node")])
    pos = pos.astype(jnp.int32)
    inputs = saved_inputs[0, 0]
    proj_in = w_in[0]
    proj_out = w_out[0]

    *packed, code = call(
        dispatch_kernel,
        [shape(PACKED, LANES)] * SENDS + [shape(TOK, 2, dtype=jnp.int32)],
        [SMEM] + [VMEM] * 3,
        pos,
        expert_ids.T,
        gates.T,
        grad_out,
    )
    landed = [lax.ppermute(p, ("rep", "exp"), send_pairs(k)) for k, p in zip(ORDER, packed)]

    act, slope, wide = call(
        hidden_kernel,
        [shape(SLOTS, HID), shape(SLOTS, HID, dtype=jnp.float32), shape(WIDTH, SLOTS)],
        [SMEM] + [VMEM] * 2,
        pos,
        inputs,
        proj_in,
    )

    *landed, slope, wide, act = lax.optimization_barrier((*landed, slope, wide, act))
    shares = call(unpack_kernel, shape(REP, SHARE, WIDTH), [VMEM] * SENDS, *landed)
    got = lax.all_to_all(shares, "rep", 0, 0, tiled=True).reshape(SLOTS, WIDTH)
    dhid, terms = call(
        middle_kernel,
        [shape(SLOTS, HID), shape(NODE, 2 * ROWS, HID)],
        [VMEM] * 5,
        got,
        wide,
        act,
        proj_out,
        slope,
        scratch=[
            pltpu.VMEM((NODE, 2 * ROWS, HID), jnp.bfloat16),
            pltpu.SemaphoreType.DMA((NODE,)),
        ],
        out_specs=[VMEM, HBM],
    )
    summed = lax.psum_scatter(
        terms.reshape(NODE * 2 * ROWS, HID), "node", scatter_dimension=0, tiled=True
    )
    part = call(part_kernel, shape(X, PAIR, PART, LANES), [VMEM] * 2, dhid, proj_in)
    part = lax.all_to_all(part, "rep", 0, 0, axis_index_groups=ALONG_X, tiled=True)
    keep, send = call(
        sum_kernel,
        [shape(PART, LANES, dtype=jnp.float32), shape(PART, LANES)],
        [SMEM, VMEM],
        pos,
        part,
    )
    other = lax.ppermute(send, "rep", NEIGHBOUR)
    back = call(back_kernel, shape(EXP * BACK, LANES), [SMEM] + [VMEM] * 2, pos, keep, other)
    back = lax.all_to_all(back.reshape(EXP, BACK, LANES), "exp", 0, 0, tiled=True)
    grad_inputs = call(
        combine_kernel, shape(COLS, TOK), [VMEM] * 2, code, back.reshape(EXP * BACK, LANES)
    )
    grad_w_in, grad_w_out = call(
        split_kernel,
        [shape(ROWS, HID)] * 2,
        [HBM],
        summed,
        scratch=[pltpu.SemaphoreType.DMA((2,))],
        out_specs=[HBM] * 2,
    )
    return grad_inputs.T, grad_w_in[None], grad_w_out[None]


def solution(mesh):
    return jax.shard_map(
        local,
        mesh=mesh,
        in_specs=(
            P(("exp", "node"), None),
            P(("exp", "node"), None),
            P(("exp", "node"), None),
            P("exp", "node", None, None),
            P("exp", None, "rep"),
            P("exp", None, "rep"),
        ),
        out_specs=(P(("exp", "node"), "rep"), P("exp", "node", "rep"), P("exp", "node", "rep")),
        check_vma=False,
    )
```

```python
import jax
import jax.numpy as jnp
from jax import lax
from jax.experimental import pallas as pl
from jax.experimental.pallas import tpu as pltpu
from jax.sharding import PartitionSpec as P

SQRT_HALF = 0.7071067811865476
INV_ROOT_TAU = 0.3989422804014327

REP, EXP, NODE = 8, 32, 4
X, PAIR = 4, 2
ALONG_X = [[PAIR * x + y for x in range(X)] for y in range(PAIR)]
NEIGHBOUR = [(r, r ^ 1) for r in range(REP)]
TOK, WIDTH, CAP = 128, 1664, 10
SLOTS = EXP * CAP
HID = 512
LANES = 128
TILES = WIDTH // LANES
COLS = WIDTH // REP
ROWS = WIDTH // NODE
SENDS = EXP // REP
PACKED = 136
BACK = 24
HALF = LANES // 2
PART = 528
SHARE = SENDS * CAP
ORDER = (2, 1, 3, 0)

VMEM = pl.BlockSpec(memory_space=pltpu.VMEM)
SMEM = pl.BlockSpec(memory_space=pltpu.SMEM)
HBM = pl.BlockSpec(memory_space=pltpu.HBM)
BUSY = pl.CostEstimate(flops=2 * 10**9, transcendentals=0, bytes_accessed=10**6)
PARAMS = pltpu.CompilerParams(vmem_limit_bytes=48 * 1024 * 1024)


def iota(shape, dim):
    return lax.broadcasted_iota(jnp.int32, shape, dim)


def hot(mask):
    return jnp.where(mask, 1.0, 0.0).astype(jnp.bfloat16)


def dot(a, b, dims=((1,), (0,))):
    return lax.dot_general(a, b, (dims, ((), ())), preferred_element_type=jnp.float32)


def in_order(k):
    step = jnp.full_like(k, ORDER[0])
    for q in range(1, SENDS):
        step = jnp.where(k == q, ORDER[q], step)
    return step


def table_kernel(ids_ref, code_ref, target_ref):
    lane = iota((TOK, LANES), 1)
    before = hot(iota((TOK, TOK), 0) > iota((TOK, TOK), 1))
    ids = jnp.concatenate([ids_ref[...], jnp.zeros((6, TOK), jnp.int32)], axis=0).T
    first = ids[:, 0:1]
    second = ids[:, 1:2]
    hot0 = hot(first == lane)
    hot1 = hot(second == lane)
    count0 = jnp.sum(hot0.astype(jnp.float32), axis=0, keepdims=True)
    rank0 = dot(before, hot0)
    rank1 = dot(before, hot1) + count0
    slot0 = jnp.sum(rank0 * hot0.astype(jnp.float32), axis=1, keepdims=True).astype(jnp.int32)
    slot1 = jnp.sum(rank1 * hot1.astype(jnp.float32), axis=1, keepdims=True).astype(jnp.int32)
    kept0 = slot0 < CAP
    kept1 = slot1 < CAP
    code_ref[:, 0:1] = jnp.where(kept0, first * BACK + slot0, -100)
    code_ref[:, 1:2] = jnp.where(kept1, second * BACK + slot1, -100)
    target_ref[:, 0:1] = jnp.where(kept0, first * 16 + slot0, -1)
    target_ref[:, 1:2] = jnp.where(kept1, second * 16 + slot1, -1)


def dispatch_kernel(pos_ref, target_ref, gates_ref, grad_ref, o0, o1, o2, o3):
    rep, src = pos_ref[0], pos_ref[1]
    target0 = target_ref[:, 0:1]
    target1 = target_ref[:, 1:2]
    gates = jnp.concatenate([gates_ref[...], jnp.zeros((6, TOK), jnp.float32)], axis=0).T
    col = iota((1, LANES), 1)
    k = col >> 4
    c = col & 15
    expert = ((rep - src) & 7) + 8 * (((src >> 3) + in_order(k)) & 3)
    wanted = jnp.where((c < CAP) & (k < SENDS), expert * 16 + c, -2)
    grad = grad_ref[...].astype(jnp.float32)
    scaled0 = (gates[:, 0:1] * grad).astype(jnp.bfloat16)
    scaled1 = (gates[:, 1:2] * grad).astype(jnp.bfloat16)
    rows = dot(hot(target0 == wanted), scaled0, ((0,), (0,))) + dot(
        hot(target1 == wanted), scaled1, ((0,), (0,))
    )
    rows = rows.astype(jnp.bfloat16)
    stacked = jnp.concatenate(
        [
            jnp.concatenate(
                [rows[16 * q : 16 * q + 16, LANES * t : LANES * (t + 1)] for q in range(SENDS)],
                axis=1,
            )
            for t in range(TILES)
        ],
        axis=0,
    )
    i = iota((PACKED, 16 * TILES), 1)
    squeeze = hot((iota((PACKED, 16 * TILES), 0) == (i >> 4) * CAP + (i & 15)) & ((i & 15) < CAP))
    packed = dot(squeeze, stacked).astype(jnp.bfloat16)
    for q, out in enumerate((o0, o1, o2, o3)):
        out[...] = packed[:, LANES * q : LANES * (q + 1)]


def unpack_kernel(i0, i1, i2, i3, out_ref):
    packed = jnp.concatenate([ref[...] for ref in (i0, i1, i2, i3)], axis=1)
    i = iota((16 * TILES, PACKED), 0)
    spread = hot((iota((16 * TILES, PACKED), 1) == (i >> 4) * CAP + (i & 15)) & ((i & 15) < CAP))
    stacked = dot(spread, packed).astype(jnp.bfloat16)
    rows = jnp.concatenate(
        [
            jnp.concatenate(
                [stacked[16 * t : 16 * t + 16, LANES * q : LANES * (q + 1)] for t in range(TILES)],
                axis=1,
            )
            for q in range(SENDS)
        ],
        axis=0,
    )
    j = iota((SHARE, 16 * SENDS), 0)
    k = lax.div(j, CAP)
    dense = hot(iota((SHARE, 16 * SENDS), 1) == k * 16 + (j - k * CAP))
    share = dot(dense, rows).astype(jnp.bfloat16)
    for q in range(REP):
        out_ref[q] = share


def fold(rows):
    half = rows.shape[0] // 2
    return jnp.concatenate([rows[:half], rows[half:]], axis=1)


def unfold(rows):
    return jnp.concatenate([rows[:, :HALF], rows[:, HALF:]], axis=0)


def places(exp):
    j = iota((1, SLOTS), 1)
    block = lax.div(j, SHARE)
    rest = j - block * SHARE
    k = lax.div(rest, CAP)
    source = ((block - exp) & 7) + 8 * (((exp >> 3) - in_order(k)) & 3)
    return source * CAP + (rest - k * CAP)


def hidden_kernel(pos_ref, inputs_ref, w_in_ref, act_ref, slope_ref, wide_ref):
    order = hot(iota((SLOTS, SLOTS), 0) == places(pos_ref[1]))
    inputs = dot(order, inputs_ref[...], ((0,), (0,))).astype(jnp.bfloat16)
    hidden = dot(inputs, w_in_ref[...])
    cdf = 0.5 * (1.0 + lax.erf(hidden * SQRT_HALF))
    act_ref[...] = (hidden * cdf).astype(jnp.bfloat16)
    slope_ref[...] = cdf + hidden * INV_ROOT_TAU * jnp.exp(-0.5 * hidden * hidden)
    wide_ref[...] = inputs.T


def middle_kernel(
    got_ref, wide_ref, act_ref, w_out_ref, slope_ref, dhid_ref, terms_hbm, terms_ref, sems
):
    up = got_ref[...]
    dhid = (dot(up, w_out_ref[...]) * slope_ref[...]).astype(jnp.bfloat16)
    dhid_ref[...] = dhid
    term = dot(up, act_ref[...], ((0,), (0,)))
    copies = []
    for q in range(NODE):
        rows = slice(ROWS * q, ROWS * (q + 1))
        terms_ref[q, ROWS:] = term[rows].astype(jnp.bfloat16)
        terms_ref[q, :ROWS] = dot(wide_ref[rows, :], dhid).astype(jnp.bfloat16)
        copies.append(pltpu.make_async_copy(terms_ref.at[q], terms_hbm.at[q], sems.at[q]))
        copies[-1].start()
    for copy in copies:
        copy.wait()


def split_kernel(summed_hbm, in_hbm, out_hbm, sems):
    copies = [
        pltpu.make_async_copy(summed_hbm.at[:ROWS], in_hbm, sems.at[0]),
        pltpu.make_async_copy(summed_hbm.at[ROWS:], out_hbm, sems.at[1]),
    ]
    for copy in copies:
        copy.start()
    for copy in copies:
        copy.wait()


def part_kernel(dhid_ref, w_in_ref, part_ref):
    dhid = dhid_ref[...]
    for q in range(REP):
        block = dot(w_in_ref[COLS * q : COLS * (q + 1), :], dhid, ((1,), (1,)))
        x, y = divmod(q, PAIR)
        part_ref[x, y, 0:COLS] = block[:, :LANES].astype(jnp.bfloat16)
        part_ref[x, y, COLS : 2 * COLS] = block[:, LANES : 2 * LANES].astype(jnp.bfloat16)
        last = fold(block[:, 2 * LANES :])
        last = jnp.concatenate([last, jnp.zeros((8, LANES), jnp.float32)], axis=0)
        part_ref[x, y, 2 * COLS :] = last.astype(jnp.bfloat16)


def sum_kernel(pos_ref, part_ref, keep_ref, send_ref):
    mine = pos_ref[0] & 1
    keep = part_ref[0, mine].astype(jnp.float32)
    send = part_ref[0, 1 - mine].astype(jnp.float32)
    for q in range(1, X):
        keep = keep + part_ref[q, mine].astype(jnp.float32)
        send = send + part_ref[q, 1 - mine].astype(jnp.float32)
    keep_ref[...] = keep
    send_ref[...] = send.astype(jnp.bfloat16)


def back_kernel(pos_ref, keep_ref, other_ref, out_ref):
    total = keep_ref[...] + other_ref[...].astype(jnp.float32)
    last = unfold(total[2 * COLS : 2 * COLS + COLS // 2])
    total = jnp.concatenate([total[:COLS], total[COLS : 2 * COLS]], axis=1)
    total = jnp.concatenate([total, last], axis=1)
    total = jnp.concatenate([total, jnp.zeros((2 * LANES - COLS, SLOTS), jnp.float32)], axis=0)
    total = total.astype(jnp.bfloat16)
    m = iota((EXP * BACK, SLOTS), 0)
    s = lax.div(m, BACK)
    q = m - s * BACK
    place = places(pos_ref[1])
    one = hot((place == s * CAP + q) & (q < CAP))
    two = hot((place == s * CAP + q - CAP) & (q >= CAP) & (q < 2 * CAP))
    out = dot(one, total[:LANES], ((1,), (1,))) + dot(two, total[LANES:], ((1,), (1,)))
    out_ref[...] = out.astype(jnp.bfloat16)


def combine_kernel(code_ref, back_ref, out_ref):
    lane = iota((TOK, EXP * BACK), 1)
    code0 = code_ref[:, 0:1]
    code1 = code_ref[:, 1:2]
    back = back_ref[...]
    head = dot(back, hot((lane == code0) | (lane == code1)), ((0,), (1,)))
    tail = dot(back, hot((lane == code0 + CAP) | (lane == code1 + CAP)), ((0,), (1,)))
    out_ref[:LANES] = head.astype(jnp.bfloat16)
    out_ref[LANES:] = tail[: COLS - LANES].astype(jnp.bfloat16)


def call(kernel, out, in_specs, *args, scratch=(), out_specs=None, cost=None):
    return pl.pallas_call(
        kernel,
        out_shape=out,
        in_specs=in_specs,
        out_specs=out_specs or jax.tree.map(lambda _: VMEM, out),
        scratch_shapes=list(scratch),
        compiler_params=PARAMS,
        cost_estimate=cost,
    )(*args)


def shape(*dims, dtype=jnp.bfloat16):
    return jax.ShapeDtypeStruct(dims, dtype)


def send_pairs(k):
    pairs = []
    for rep in range(REP):
        for src in range(EXP):
            dst = (rep - src) % 8 + 8 * ((src // 8 + k) % SENDS)
            pairs.append((rep * EXP + src, rep * EXP + dst))
    return pairs


def local(grad_out, gates, expert_ids, saved_inputs, w_in, w_out):
    pos = jnp.stack([lax.axis_index("rep"), lax.axis_index("exp"), lax.axis_index("node")])
    pos = pos.astype(jnp.int32)
    inputs = saved_inputs[0, 0]
    proj_in = w_in[0]
    proj_out = w_out[0]

    code, target = call(table_kernel, [shape(TOK, 2, dtype=jnp.int32)] * 2, [VMEM], expert_ids.T, cost=BUSY)
    packed = call(
        dispatch_kernel,
        [shape(PACKED, LANES)] * SENDS,
        [SMEM] + [VMEM] * 3,
        pos,
        target,
        gates.T,
        grad_out,
        cost=BUSY,
    )
    landed = [lax.ppermute(p, ("rep", "exp"), send_pairs(k)) for k, p in zip(ORDER, packed)]

    act, slope, wide = call(
        hidden_kernel,
        [shape(SLOTS, HID), shape(SLOTS, HID, dtype=jnp.float32), shape(WIDTH, SLOTS)],
        [SMEM] + [VMEM] * 2,
        pos,
        inputs,
        proj_in,
    )

    *landed, slope, wide, act = lax.optimization_barrier((*landed, slope, wide, act))
    shares = call(unpack_kernel, shape(REP, SHARE, WIDTH), [VMEM] * SENDS, *landed)
    got = lax.all_to_all(shares, "rep", 0, 0, tiled=True).reshape(SLOTS, WIDTH)
    dhid, terms = call(
        middle_kernel,
        [shape(SLOTS, HID), shape(NODE, 2 * ROWS, HID)],
        [VMEM] * 5,
        got,
        wide,
        act,
        proj_out,
        slope,
        scratch=[
            pltpu.VMEM((NODE, 2 * ROWS, HID), jnp.bfloat16),
            pltpu.SemaphoreType.DMA((NODE,)),
        ],
        out_specs=[VMEM, HBM],
        cost=BUSY,
    )
    summed = lax.psum_scatter(
        terms.reshape(NODE * 2 * ROWS, HID), "node", scatter_dimension=0, tiled=True
    )
    part = call(part_kernel, shape(X, PAIR, PART, LANES), [VMEM] * 2, dhid, proj_in)
    part = lax.all_to_all(part, "rep", 0, 0, axis_index_groups=ALONG_X, tiled=True)
    keep, send = call(
        sum_kernel,
        [shape(PART, LANES, dtype=jnp.float32), shape(PART, LANES)],
        [SMEM, VMEM],
        pos,
        part,
    )
    other = lax.ppermute(send, "rep", NEIGHBOUR)
    back = call(back_kernel, shape(EXP * BACK, LANES), [SMEM] + [VMEM] * 2, pos, keep, other)
    back = lax.all_to_all(back.reshape(EXP, BACK, LANES), "exp", 0, 0, tiled=True)
    grad_inputs = call(
        combine_kernel, shape(COLS, TOK), [VMEM] * 2, code, back.reshape(EXP * BACK, LANES)
    )
    grad_w_in, grad_w_out = call(
        split_kernel,
        [shape(ROWS, HID)] * 2,
        [HBM],
        summed,
        scratch=[pltpu.SemaphoreType.DMA((2,))],
        out_specs=[HBM] * 2,
    )
    return grad_inputs.T, grad_w_in[None], grad_w_out[None]


def solution(mesh):
    return jax.shard_map(
        local,
        mesh=mesh,
        in_specs=(
            P(("exp", "node"), None),
            P(("exp", "node"), None),
            P(("exp", "node"), None),
            P("exp", "node", None, None),
            P("exp", None, "rep"),
            P("exp", None, "rep"),
        ),
        out_specs=(P(("exp", "node"), "rep"), P("exp", "node", "rep"), P("exp", "node", "rep")),
        check_vma=False,
    )
```

```python
import jax
import jax.numpy as jnp
from jax import lax
from jax.experimental import pallas as pl
from jax.experimental.pallas import tpu as pltpu
from jax.sharding import PartitionSpec as P

SQRT_HALF = 0.7071067811865476
INV_ROOT_TAU = 0.3989422804014327

REP, EXP, NODE = 8, 32, 4
X, PAIR = 4, 2
ALONG_X = [[PAIR * x + y for x in range(X)] for y in range(PAIR)]
NEIGHBOUR = [(r, r ^ 1) for r in range(REP)]
TOK, WIDTH, CAP = 128, 1664, 10
SLOTS = EXP * CAP
HID = 512
LANES = 128
TILES = WIDTH // LANES
COLS = WIDTH // REP
ROWS = WIDTH // NODE
SENDS = EXP // REP
PACKED = 136
BACK = 24
HALF = LANES // 2
PART = 528
SHARE = SENDS * CAP
ORDER = (1, 3, 2, 0)

VMEM = pl.BlockSpec(memory_space=pltpu.VMEM)
SMEM = pl.BlockSpec(memory_space=pltpu.SMEM)
HBM = pl.BlockSpec(memory_space=pltpu.HBM)
BUSY = pl.CostEstimate(flops=2 * 10**9, transcendentals=0, bytes_accessed=10**6)
PARAMS = pltpu.CompilerParams(vmem_limit_bytes=48 * 1024 * 1024)


def iota(shape, dim):
    return lax.broadcasted_iota(jnp.int32, shape, dim)


def hot(mask):
    return jnp.where(mask, 1.0, 0.0).astype(jnp.bfloat16)


def dot(a, b, dims=((1,), (0,))):
    return lax.dot_general(a, b, (dims, ((), ())), preferred_element_type=jnp.float32)


def in_order(k):
    step = jnp.full_like(k, ORDER[0])
    for q in range(1, SENDS):
        step = jnp.where(k == q, ORDER[q], step)
    return step


def table_kernel(ids_ref, code_ref, target_ref):
    lane = iota((TOK, LANES), 1)
    before = hot(iota((TOK, TOK), 0) > iota((TOK, TOK), 1))
    ids = jnp.concatenate([ids_ref[...], jnp.zeros((6, TOK), jnp.int32)], axis=0).T
    first = ids[:, 0:1]
    second = ids[:, 1:2]
    hot0 = hot(first == lane)
    hot1 = hot(second == lane)
    count0 = jnp.sum(hot0.astype(jnp.float32), axis=0, keepdims=True)
    rank0 = dot(before, hot0)
    rank1 = dot(before, hot1) + count0
    slot0 = jnp.sum(rank0 * hot0.astype(jnp.float32), axis=1, keepdims=True).astype(jnp.int32)
    slot1 = jnp.sum(rank1 * hot1.astype(jnp.float32), axis=1, keepdims=True).astype(jnp.int32)
    kept0 = slot0 < CAP
    kept1 = slot1 < CAP
    code_ref[:, 0:1] = jnp.where(kept0, first * BACK + slot0, -100)
    code_ref[:, 1:2] = jnp.where(kept1, second * BACK + slot1, -100)
    target_ref[:, 0:1] = jnp.where(kept0, first * 16 + slot0, -1)
    target_ref[:, 1:2] = jnp.where(kept1, second * 16 + slot1, -1)


def dispatch_kernel(pos_ref, target_ref, gates_ref, grad_ref, o0, o1, o2, o3):
    rep, src = pos_ref[0], pos_ref[1]
    target0 = target_ref[:, 0:1]
    target1 = target_ref[:, 1:2]
    gates = jnp.concatenate([gates_ref[...], jnp.zeros((6, TOK), jnp.float32)], axis=0).T
    col = iota((1, LANES), 1)
    k = col >> 4
    c = col & 15
    expert = ((rep - src) & 7) + 8 * (((src >> 3) + in_order(k)) & 3)
    wanted = jnp.where((c < CAP) & (k < SENDS), expert * 16 + c, -2)
    grad = grad_ref[...].astype(jnp.float32)
    scaled0 = (gates[:, 0:1] * grad).astype(jnp.bfloat16)
    scaled1 = (gates[:, 1:2] * grad).astype(jnp.bfloat16)
    rows = dot(hot(target0 == wanted), scaled0, ((0,), (0,))) + dot(
        hot(target1 == wanted), scaled1, ((0,), (0,))
    )
    rows = rows.astype(jnp.bfloat16)
    stacked = jnp.concatenate(
        [
            jnp.concatenate(
                [rows[16 * q : 16 * q + 16, LANES * t : LANES * (t + 1)] for q in range(SENDS)],
                axis=1,
            )
            for t in range(TILES)
        ],
        axis=0,
    )
    i = iota((PACKED, 16 * TILES), 1)
    squeeze = hot((iota((PACKED, 16 * TILES), 0) == (i >> 4) * CAP + (i & 15)) & ((i & 15) < CAP))
    packed = dot(squeeze, stacked).astype(jnp.bfloat16)
    for q, out in enumerate((o0, o1, o2, o3)):
        out[...] = packed[:, LANES * q : LANES * (q + 1)]


def unpack_kernel(i0, i1, i2, i3, out_ref):
    packed = jnp.concatenate([ref[...] for ref in (i0, i1, i2, i3)], axis=1)
    i = iota((16 * TILES, PACKED), 0)
    spread = hot((iota((16 * TILES, PACKED), 1) == (i >> 4) * CAP + (i & 15)) & ((i & 15) < CAP))
    stacked = dot(spread, packed).astype(jnp.bfloat16)
    rows = jnp.concatenate(
        [
            jnp.concatenate(
                [stacked[16 * t : 16 * t + 16, LANES * q : LANES * (q + 1)] for t in range(TILES)],
                axis=1,
            )
            for q in range(SENDS)
        ],
        axis=0,
    )
    j = iota((SHARE, 16 * SENDS), 0)
    k = lax.div(j, CAP)
    dense = hot(iota((SHARE, 16 * SENDS), 1) == k * 16 + (j - k * CAP))
    share = dot(dense, rows).astype(jnp.bfloat16)
    for q in range(REP):
        out_ref[q] = share


def fold(rows):
    half = rows.shape[0] // 2
    return jnp.concatenate([rows[:half], rows[half:]], axis=1)


def unfold(rows):
    return jnp.concatenate([rows[:, :HALF], rows[:, HALF:]], axis=0)


def places(exp):
    j = iota((1, SLOTS), 1)
    block = lax.div(j, SHARE)
    rest = j - block * SHARE
    k = lax.div(rest, CAP)
    source = ((block - exp) & 7) + 8 * (((exp >> 3) - in_order(k)) & 3)
    return source * CAP + (rest - k * CAP)


def hidden_kernel(pos_ref, inputs_ref, w_in_ref, act_ref, slope_ref, wide_ref):
    order = hot(iota((SLOTS, SLOTS), 0) == places(pos_ref[1]))
    inputs = dot(order, inputs_ref[...], ((0,), (0,))).astype(jnp.bfloat16)
    hidden = dot(inputs, w_in_ref[...])
    cdf = 0.5 * (1.0 + lax.erf(hidden * SQRT_HALF))
    act_ref[...] = (hidden * cdf).astype(jnp.bfloat16)
    slope_ref[...] = cdf + hidden * INV_ROOT_TAU * jnp.exp(-0.5 * hidden * hidden)
    wide_ref[...] = inputs.T


def middle_kernel(
    got_ref, wide_ref, act_ref, w_out_ref, slope_ref, dhid_ref, terms_hbm, terms_ref, sems
):
    up = got_ref[...]
    dhid = (dot(up, w_out_ref[...]) * slope_ref[...]).astype(jnp.bfloat16)
    dhid_ref[...] = dhid
    term = dot(up, act_ref[...], ((0,), (0,)))
    copies = []
    for q in range(NODE):
        rows = slice(ROWS * q, ROWS * (q + 1))
        terms_ref[q, ROWS:] = term[rows].astype(jnp.bfloat16)
        terms_ref[q, :ROWS] = dot(wide_ref[rows, :], dhid).astype(jnp.bfloat16)
        copies.append(pltpu.make_async_copy(terms_ref.at[q], terms_hbm.at[q], sems.at[q]))
        copies[-1].start()
    for copy in copies:
        copy.wait()


def split_kernel(summed_hbm, in_hbm, out_hbm, sems):
    copies = [
        pltpu.make_async_copy(summed_hbm.at[:ROWS], in_hbm, sems.at[0]),
        pltpu.make_async_copy(summed_hbm.at[ROWS:], out_hbm, sems.at[1]),
    ]
    for copy in copies:
        copy.start()
    for copy in copies:
        copy.wait()


def part_kernel(dhid_ref, w_in_ref, part_ref):
    dhid = dhid_ref[...]
    for q in range(REP):
        block = dot(w_in_ref[COLS * q : COLS * (q + 1), :], dhid, ((1,), (1,)))
        x, y = divmod(q, PAIR)
        part_ref[x, y, 0:COLS] = block[:, :LANES].astype(jnp.bfloat16)
        part_ref[x, y, COLS : 2 * COLS] = block[:, LANES : 2 * LANES].astype(jnp.bfloat16)
        last = fold(block[:, 2 * LANES :])
        last = jnp.concatenate([last, jnp.zeros((8, LANES), jnp.float32)], axis=0)
        part_ref[x, y, 2 * COLS :] = last.astype(jnp.bfloat16)


def sum_kernel(pos_ref, part_ref, keep_ref, send_ref):
    mine = pos_ref[0] & 1
    keep = part_ref[0, mine].astype(jnp.float32)
    send = part_ref[0, 1 - mine].astype(jnp.float32)
    for q in range(1, X):
        keep = keep + part_ref[q, mine].astype(jnp.float32)
        send = send + part_ref[q, 1 - mine].astype(jnp.float32)
    keep_ref[...] = keep
    send_ref[...] = send.astype(jnp.bfloat16)


def back_kernel(pos_ref, keep_ref, other_ref, out_ref):
    total = keep_ref[...] + other_ref[...].astype(jnp.float32)
    last = unfold(total[2 * COLS : 2 * COLS + COLS // 2])
    total = jnp.concatenate([total[:COLS], total[COLS : 2 * COLS]], axis=1)
    total = jnp.concatenate([total, last], axis=1)
    total = jnp.concatenate([total, jnp.zeros((2 * LANES - COLS, SLOTS), jnp.float32)], axis=0)
    total = total.astype(jnp.bfloat16)
    m = iota((EXP * BACK, SLOTS), 0)
    s = lax.div(m, BACK)
    q = m - s * BACK
    place = places(pos_ref[1])
    one = hot((place == s * CAP + q) & (q < CAP))
    two = hot((place == s * CAP + q - CAP) & (q >= CAP) & (q < 2 * CAP))
    out = dot(one, total[:LANES], ((1,), (1,))) + dot(two, total[LANES:], ((1,), (1,)))
    out_ref[...] = out.astype(jnp.bfloat16)


def combine_kernel(code_ref, back_ref, out_ref):
    lane = iota((TOK, EXP * BACK), 1)
    code0 = code_ref[:, 0:1]
    code1 = code_ref[:, 1:2]
    back = back_ref[...]
    head = dot(back, hot((lane == code0) | (lane == code1)), ((0,), (1,)))
    tail = dot(back, hot((lane == code0 + CAP) | (lane == code1 + CAP)), ((0,), (1,)))
    out_ref[:LANES] = head.astype(jnp.bfloat16)
    out_ref[LANES:] = tail[: COLS - LANES].astype(jnp.bfloat16)


def call(kernel, out, in_specs, *args, scratch=(), out_specs=None, cost=None):
    return pl.pallas_call(
        kernel,
        out_shape=out,
        in_specs=in_specs,
        out_specs=out_specs or jax.tree.map(lambda _: VMEM, out),
        scratch_shapes=list(scratch),
        compiler_params=PARAMS,
        cost_estimate=cost,
    )(*args)


def shape(*dims, dtype=jnp.bfloat16):
    return jax.ShapeDtypeStruct(dims, dtype)


def send_pairs(k):
    pairs = []
    for rep in range(REP):
        for src in range(EXP):
            dst = (rep - src) % 8 + 8 * ((src // 8 + k) % SENDS)
            pairs.append((rep * EXP + src, rep * EXP + dst))
    return pairs


def local(grad_out, gates, expert_ids, saved_inputs, w_in, w_out):
    pos = jnp.stack([lax.axis_index("rep"), lax.axis_index("exp"), lax.axis_index("node")])
    pos = pos.astype(jnp.int32)
    inputs = saved_inputs[0, 0]
    proj_in = w_in[0]
    proj_out = w_out[0]

    code, target = call(table_kernel, [shape(TOK, 2, dtype=jnp.int32)] * 2, [VMEM], expert_ids.T, cost=BUSY)
    packed = call(
        dispatch_kernel,
        [shape(PACKED, LANES)] * SENDS,
        [SMEM] + [VMEM] * 3,
        pos,
        target,
        gates.T,
        grad_out,
        cost=BUSY,
    )
    landed = [lax.ppermute(p, ("rep", "exp"), send_pairs(k)) for k, p in zip(ORDER, packed)]

    act, slope, wide = call(
        hidden_kernel,
        [shape(SLOTS, HID), shape(SLOTS, HID, dtype=jnp.float32), shape(WIDTH, SLOTS)],
        [SMEM] + [VMEM] * 2,
        pos,
        inputs,
        proj_in,
    )

    *landed, slope, wide, act = lax.optimization_barrier((*landed, slope, wide, act))
    shares = call(unpack_kernel, shape(REP, SHARE, WIDTH), [VMEM] * SENDS, *landed)
    got = lax.all_to_all(shares, "rep", 0, 0, tiled=True).reshape(SLOTS, WIDTH)
    dhid, terms = call(
        middle_kernel,
        [shape(SLOTS, HID), shape(NODE, 2 * ROWS, HID)],
        [VMEM] * 5,
        got,
        wide,
        act,
        proj_out,
        slope,
        scratch=[
            pltpu.VMEM((NODE, 2 * ROWS, HID), jnp.bfloat16),
            pltpu.SemaphoreType.DMA((NODE,)),
        ],
        out_specs=[VMEM, HBM],
        cost=BUSY,
    )
    summed = lax.psum_scatter(
        terms.reshape(NODE * 2 * ROWS, HID), "node", scatter_dimension=0, tiled=True
    )
    part = call(part_kernel, shape(X, PAIR, PART, LANES), [VMEM] * 2, dhid, proj_in)
    part = lax.all_to_all(part, "rep", 0, 0, axis_index_groups=ALONG_X, tiled=True)
    keep, send = call(
        sum_kernel,
        [shape(PART, LANES, dtype=jnp.float32), shape(PART, LANES)],
        [SMEM, VMEM],
        pos,
        part,
    )
    other = lax.ppermute(send, "rep", NEIGHBOUR)
    back = call(back_kernel, shape(EXP * BACK, LANES), [SMEM] + [VMEM] * 2, pos, keep, other)
    back = lax.all_to_all(back.reshape(EXP, BACK, LANES), "exp", 0, 0, tiled=True)
    grad_inputs = call(
        combine_kernel, shape(COLS, TOK), [VMEM] * 2, code, back.reshape(EXP * BACK, LANES)
    )
    grad_w_in, grad_w_out = call(
        split_kernel,
        [shape(ROWS, HID)] * 2,
        [HBM],
        summed,
        scratch=[pltpu.SemaphoreType.DMA((2,))],
        out_specs=[HBM] * 2,
    )
    return grad_inputs.T, grad_w_in[None], grad_w_out[None]


def solution(mesh):
    return jax.shard_map(
        local,
        mesh=mesh,
        in_specs=(
            P(("exp", "node"), None),
            P(("exp", "node"), None),
            P(("exp", "node"), None),
            P("exp", "node", None, None),
            P("exp", None, "rep"),
            P("exp", None, "rep"),
        ),
        out_specs=(P(("exp", "node"), "rep"), P("exp", "node", "rep"), P("exp", "node", "rep")),
        check_vma=False,
    )
```
